32 devices in a mesh: row: 4 (over z), col: 8 (over y, x, core).
Axes of the slice: x: 2, y: 2, z: 4, core: 2. Of those that a mesh axis runs over, the one named last changes fastest.
Arguments:
- hidden_input: bfloat16 [4096, 1536], P(('row', 'col')), may hold values from -6 to 6
- lengths: int32 [4, 4], replicated, may hold values from 1 to 768, 1024 in all within a row
- prompt_adapter: int32 [4, 4], replicated, may hold values from 0 to 31
- routes: int32 [4096, 4], P(('row', 'col')), may hold values from 0 to 15, all different within a row; in each aligned block of 128 rows (0 to 127, 128 to 255, ...) at most 40 rows name the same one
- attention_norm_gain: bfloat16 [1536], replicated, may hold values from 0.5 to 1.5
- expert_norm_gain: bfloat16 [1536], replicated, may hold values from 0.5 to 1.5
- projection_weight: bfloat16 [1536, 2048], P('row', 'col')
- output_weight: bfloat16 [1536, 1536], P('row', 'col'), may hold values from -0.15625 to 0.15625
- router: bfloat16 [1536, 16], replicated, may hold values from -0.5 to 0.5
- adapter_projection_down: bfloat16 [32, 16, 1536], P('col'), may hold values from -0.15625 to 0.15625
- adapter_projection_up: bfloat16 [32, 16, 2048], P('col'), may hold values from -1.5 to 1.5
- adapter_output_down: bfloat16 [32, 16, 1536], P('col'), may hold values from -0.15625 to 0.15625
- adapter_output_up: bfloat16 [32, 16, 1536], P('col'), may hold values from -1.5 to 1.5
- expert_gate_weight: bfloat16 [16, 1536, 768], P('col'), may hold values from -0.15625 to 0.15625
- expert_up_weight: bfloat16 [16, 1536, 768], P('col'), may hold values from -0.15625 to 0.15625
- expert_down_weight: bfloat16 [16, 768, 1536], P('col'), may hold values from -0.21875 to 0.21875
Outputs:
- hidden_out: bfloat16 [4096, 1536], P(('row', 'col'))
The draws below stay inside these ranges and needn't reach their ends.
Inputs may be any that keep to these rules, and one draw needn't show every extreme that they name: The 4 lengths of a block sum to 1024; in every block the longest prompt has exactly 768 tokens. `prompt_adapter`: adapter a is held by index a // 4 of col. `routes`: the 4 experts of a token differ; among the rows of one device no expert is named more than 40 times, a bound that some block reaches. Expert e is held by index e // 2 of col.
All inputs are finite; a program needn't handle non-finite values.
Results may differ from the reference program's by a relative error of at most 0.012.
Values may be sent and summed in bfloat16 or wider, within the bound.
A program may use at most 128 MiB of HBM per device.

```python
import math
import jax
import jax.numpy as jnp
import numpy as np
from jax import lax

MODEL_DIM = 1536
QUERY_HEADS = 12
KEY_HEADS = 2
HEAD_SIZE = 128
FF = 768
TOPK = 4
ADAPTER_RANK = 16
PROMPTS = 4
TOK_DEV = 128
QUERY_PER_KEY = 6
PROJ_COLUMNS = 2048
EXPERTS = 16
ADAPTER_COUNT = 32
TOKEN_BLOCK = 1024
TOKENS = 4096
CAP = 40
N_ROW = 4


def draw_projection_weight(key, part):
    random_subkeys = jax.random.split(jax.random.fold_in(key, 7), 1)
    entire_sequence = jax.random.normal(random_subkeys[0], (MODEL_DIM, PROJ_COLUMNS), jnp.float32) / math.sqrt(MODEL_DIM)
    return entire_sequence.astype(jnp.bfloat16)


def set_ends(drawn, key, least, high):
    dims = drawn.shape
    spot = [jax.random.randint(jax.random.fold_in(key, axis), (), 0, dims[axis]) for axis in range(len(dims))]
    drawn = drawn.at[tuple(spot)].set(least)
    longest = dims.index(max(dims))
    spot[longest] = (spot[longest] + 1) % dims[longest]
    return drawn.at[tuple(spot)].set(high)


def steps_of(own_key, dims, cuts, least, high):
    def one(dim, blocks):
        heights = jax.random.uniform(jax.random.fold_in(jax.random.fold_in(own_key, 6), dim), (blocks,), jnp.float32, least / len(cuts), high / len(cuts))
        return jnp.repeat(jnp.exp(heights), dims[dim] // blocks).reshape((-1,) + (1,) * (len(dims) - dim - 1))

    factor_of = one(*cuts[0])
    for cut in cuts[1:]:
        factor_of = factor_of * one(*cut)
    return factor_of


def split_up(number_of, total, limit, lean):
    loads = [(1 << 20) // math.isqrt(standing ** lean) + 1 for standing in range(2, number_of + 1)]
    surplus, given = total - limit - (number_of - 1), [1] * (number_of - 1)
    while surplus > 0:
        free = [i for i in range(number_of - 1) if given[i] < limit]
        mass, left = sum([loads[i] for i in free]), surplus
        for i in free:
            extra = min(limit - given[i], max(1, left * loads[i] // mass), surplus)
            given[i] = given[i] + extra
            surplus = surplus - extra
    return np.array([limit] + given)


def ragged(key, amount, total, reach, skew):
    if amount == 2:
        one = jax.random.randint(key, (), max(1, total - reach), min(reach, total - 1) + 1)
        return jnp.stack([one, total - one])
    tallies = jnp.asarray(split_up(amount, total, reach, skew), jnp.int32)
    couples = (amount - 1) // 2
    source_of, taker = tallies[1:1 + 2 * couples:2], tallies[2:2 + 2 * couples:2]
    margin = jnp.minimum(source_of - 1, reach - taker)
    passed = jax.random.randint(jax.random.fold_in(key, 1), (couples,), 0, 1 << 20) % (margin + 1)
    tallies = tallies.at[1:1 + 2 * couples:2].set(source_of - passed).at[2:2 + 2 * couples:2].set(taker + passed)
    return tallies[jax.random.permutation(jax.random.fold_in(key, 2), amount)]


def assign_block(key, own, number, rows, count, top, reach, lean):
    sequence = jax.random.permutation(key, count)
    packed, common = shares(count, rows * top, reach, lean, True), shares(count, rows * top, reach, lean, False)
    places = jnp.arange(count)

    def named(sizes, offset_by):
        used = int((sizes > 0).sum())
        fixed = max(1, used // 4)
        shifted = fixed + (places - fixed + offset_by * (used - fixed)) % max(1, count - fixed)
        return jnp.zeros((count,), jnp.int32).at[sequence[jnp.where(places < fixed, places, shifted)]].set(jnp.asarray(sizes, jnp.int32))

    sizes = jnp.where(number % 4 == 0, named(packed, number // 4), named(common, number - number // 4 - 1))
    mixed = jax.random.permutation(jax.random.fold_in(own, 3), count)
    source_of, taker = mixed[0:count // 2 * 2:2], mixed[1:count // 2 * 2:2]
    room = jnp.minimum(sizes[source_of] - 1, reach - sizes[taker]) // 2
    room = jnp.where((source_of == sequence[0]) | (taker == sequence[0]) | (sizes[taker] == 0), 0, jnp.maximum(room, 0))
    shifted = jax.random.randint(jax.random.fold_in(own, 4), (count // 2,), 0, 1 << 20) % (room + 1)
    sizes = sizes.at[source_of].add(-shifted).at[taker].add(shifted)
    labels = jnp.searchsorted(jnp.cumsum(sizes), jnp.arange(rows * top), side="right").astype(jnp.int32)
    listing = labels.reshape(top, rows).T
    listing = listing[jax.random.permutation(jax.random.fold_in(own, 1), rows)]
    offset_by = jax.random.randint(jax.random.fold_in(own, 2), (rows, 1), 0, top)
    return jnp.take_along_axis(listing, (jnp.arange(top)[None, :] + offset_by) % top, axis=1)


def shares(number_of, total, most, slope, full):
    weights = [(1 << 20) // math.isqrt(standing ** slope) + 1 for standing in range(1, number_of + 1)]
    largest = most if full else min(most, max(-(-total // number_of), total * weights[0] // sum(weights)))
    least = 1 if total - largest >= number_of - 1 else 0
    holding, rest = [largest] + [least] * (number_of - 1), total - largest - least * (number_of - 1)
    while rest > 0:
        free = [i for i in range(1, number_of) if holding[i] < largest] or [i for i in range(1, number_of) if holding[i] < most]
        pool, budget = sum([weights[i] for i in free]), rest
        for i in free:
            extra = min(most - holding[i], max(1, budget * weights[i] // pool), rest)
            holding[i] = holding[i] + extra
            rest = rest - extra
    return np.array(holding)


def gaussian(key, extent, scale, bound, cuts=(), held_as=jnp.bfloat16):
    gain = steps_of(key, extent, cuts, -0.22, 0.18) if cuts else 1.0
    entries = jax.random.normal(key, extent, jnp.float32) * scale * gain
    return jnp.minimum(jnp.maximum(entries, -bound), bound).astype(held_as)


def setup_inputs(seed: int = 0) -> dict:
    key_list = jax.random.split(jax.random.key(seed), 17)
    hidden_input = gaussian(key_list[0], (TOKENS, MODEL_DIM), 1.0, 6.0, ((0, 32),))
    lengths = jax.vmap(lambda own: ragged(own, PROMPTS, TOKEN_BLOCK, 3 * TOKEN_BLOCK // 4, 2))(jax.random.split(key_list[1], N_ROW)).reshape((N_ROW, PROMPTS)).astype(jnp.int32)
    prompt_adapter = set_ends(jax.random.randint(key_list[2], (N_ROW, PROMPTS), 0, ADAPTER_COUNT), jax.random.fold_in(key_list[2], 1), 0, ADAPTER_COUNT - 1).astype(jnp.int32)
    routes_keys = jax.random.split(jax.random.fold_in(key_list[3], 1), TOKENS // TOK_DEV)
    routes_turns = jax.random.permutation(jax.random.fold_in(key_list[3], 3), TOKENS // TOK_DEV)
    routes = jax.vmap(lambda own, number: assign_block(jax.random.fold_in(key_list[3], 2), own, number, TOK_DEV, EXPERTS, TOPK, CAP, 2))(routes_keys, routes_turns).reshape((TOKENS, TOPK))
    attention_norm_gain = jnp.clip(1.0 + 0.1 * jax.random.normal(key_list[4], (MODEL_DIM,), jnp.float32), 0.5, 1.5).astype(jnp.bfloat16)
    expert_norm_gain = jnp.clip(1.0 + 0.1 * jax.random.normal(key_list[5], (MODEL_DIM,), jnp.float32), 0.5, 1.5).astype(jnp.bfloat16)
    projection_weight = draw_projection_weight(jax.random.fold_in(key_list[16], 71), 0)
    output_weight = gaussian(key_list[7], (QUERY_HEADS * HEAD_SIZE, MODEL_DIM), (QUERY_HEADS * HEAD_SIZE) ** -0.5, 0.15625, ((0, 4), (1, 8)))
    router = gaussian(key_list[8], (MODEL_DIM, EXPERTS), 0.08, 0.5)
    adapter_projection_down = gaussian(key_list[9], (ADAPTER_COUNT, ADAPTER_RANK, MODEL_DIM), MODEL_DIM ** -0.5, 0.15625, ((0, 8),))
    adapter_projection_up = gaussian(key_list[10], (ADAPTER_COUNT, ADAPTER_RANK, PROJ_COLUMNS), ADAPTER_RANK ** -0.5, 1.5, ((0, 8),))
    adapter_output_down = gaussian(key_list[11], (ADAPTER_COUNT, ADAPTER_RANK, QUERY_HEADS * HEAD_SIZE), (QUERY_HEADS * HEAD_SIZE) ** -0.5, 0.15625, ((0, 8),))
    adapter_output_up = gaussian(key_list[12], (ADAPTER_COUNT, ADAPTER_RANK, MODEL_DIM), ADAPTER_RANK ** -0.5, 1.5, ((0, 8),))
    expert_gate_weight = gaussian(key_list[13], (EXPERTS, MODEL_DIM, FF), MODEL_DIM ** -0.5, 0.15625, ((0, 8),))
    expert_up_weight = gaussian(key_list[14], (EXPERTS, MODEL_DIM, FF), MODEL_DIM ** -0.5, 0.15625, ((0, 8),))
    expert_down_weight = gaussian(key_list[15], (EXPERTS, FF, MODEL_DIM), FF ** -0.5, 0.21875, ((0, 8),))
    return {"hidden_input": hidden_input, "lengths": lengths, "prompt_adapter": prompt_adapter, "routes": routes, "attention_norm_gain": attention_norm_gain, "expert_norm_gain": expert_norm_gain, "projection_weight": projection_weight, "output_weight": output_weight, "router": router, "adapter_projection_down": adapter_projection_down, "adapter_projection_up": adapter_projection_up, "adapter_output_down": adapter_output_down, "adapter_output_up": adapter_output_up, "expert_gate_weight": expert_gate_weight, "expert_up_weight": expert_up_weight, "expert_down_weight": expert_down_weight}


norm_eps = 1e-06
rope_base = 1000000.0
adapter_scale = 0.5

def rms_scaled(value_tensor, norm_gain):
    widened = value_tensor.astype(jnp.float32)
    inverse = lax.rsqrt(lax.optimization_barrier(jnp.mean(widened * widened, axis=-1, keepdims=True)) + norm_eps)
    return (widened * inverse * norm_gain.astype(jnp.float32)).astype(jnp.bfloat16)

def prompt_layout(lengths_row, tok_index):
    prompt_ends = jnp.cumsum(lengths_row)
    starts = prompt_ends - lengths_row
    prompt_of = lax.optimization_barrier(jnp.sum((tok_index[:, None] >= prompt_ends[None, :]).astype(jnp.int32), axis=1))
    within_prompt = prompt_of[:, None] == jnp.arange(lengths_row.shape[0], dtype=jnp.int32)[None, :]
    token_positions = tok_index - lax.optimization_barrier(jnp.sum(jnp.where(within_prompt, starts[None, :], 0), axis=1))
    return (prompt_of, within_prompt, token_positions)

def apply_rotary(value_tensor, token_positions):
    half_width = value_tensor.shape[-1] // 2
    frequency = rope_base ** (-2.0 * jnp.arange(half_width, dtype=jnp.float32) / value_tensor.shape[-1])
    angles = token_positions.astype(jnp.float32)[:, None] * frequency[None, :]
    cosine = jnp.cos(angles)[:, None, :]
    sine_part = jnp.sin(angles)[:, None, :]
    front_half = value_tensor[..., :half_width]
    back_half = value_tensor[..., half_width:]
    return jnp.concatenate([front_half * cosine - back_half * sine_part, back_half * cosine + front_half * sine_part], axis=-1)

def adapter_change(inputs, within_prompt, downs, ups):
    low_rank = jnp.einsum('nk,prk->npr', inputs.astype(jnp.float32), downs.astype(jnp.float32))
    low_rank = lax.optimization_barrier(jnp.where(within_prompt[:, :, None], low_rank, 0.0).astype(jnp.bfloat16))
    return jnp.einsum('npr,pro->no', low_rank.astype(jnp.float32), ups.astype(jnp.float32))

def route_slots(flat_routes, expert_total):
    marks = (flat_routes[:, None] == jnp.arange(expert_total, dtype=jnp.int32)[None, :]).astype(jnp.int32)
    before = jnp.cumsum(marks, axis=0) - marks
    return lax.optimization_barrier(jnp.sum(before * marks, axis=1))

def reference(hidden_input, lengths, prompt_adapter, routes, attention_norm_gain, expert_norm_gain, projection_weight, output_weight, router, adapter_projection_down, adapter_projection_up, adapter_output_down, adapter_output_up, expert_gate_weight, expert_up_weight, expert_down_weight):
    blocks = hidden_input.reshape(N_ROW, TOKEN_BLOCK, MODEL_DIM)

    def attend_block(inputs):
        block_rows, lengths_row, adapter_row = inputs
        tok_index = jnp.arange(TOKEN_BLOCK, dtype=jnp.int32)
        prompt_of, within_prompt, token_positions = prompt_layout(lengths_row, tok_index)
        normalized = rms_scaled(block_rows, attention_norm_gain)
        projection_all = jnp.dot(normalized, projection_weight, preferred_element_type=jnp.float32)
        projection_all = projection_all + adapter_scale * adapter_change(normalized, within_prompt, adapter_projection_down[adapter_row], adapter_projection_up[adapter_row])
        query_rows = apply_rotary(projection_all[:, :QUERY_HEADS * HEAD_SIZE].reshape(TOKEN_BLOCK, QUERY_HEADS, HEAD_SIZE), token_positions).astype(jnp.bfloat16)
        every_key = apply_rotary(projection_all[:, QUERY_HEADS * HEAD_SIZE:(QUERY_HEADS + KEY_HEADS) * HEAD_SIZE].reshape(TOKEN_BLOCK, KEY_HEADS, HEAD_SIZE), token_positions).astype(jnp.bfloat16)
        every_value = projection_all[:, (QUERY_HEADS + KEY_HEADS) * HEAD_SIZE:].astype(jnp.bfloat16).reshape(TOKEN_BLOCK, KEY_HEADS, HEAD_SIZE)
        allowed = (prompt_of[:, None] == prompt_of[None, :]) & (tok_index[None, :] <= tok_index[:, None])
        outputs = []
        for group_number in range(KEY_HEADS):
            query_group = query_rows[:, group_number * QUERY_PER_KEY:(group_number + 1) * QUERY_PER_KEY].astype(jnp.float32).transpose(1, 0, 2)
            scores = jnp.einsum('gqd,kd->gqk', query_group, every_key[:, group_number].astype(jnp.float32)) * HEAD_SIZE ** (-0.5)
            masked = jnp.where(allowed[None], scores, -1e+30)
            highest = lax.optimization_barrier(jnp.max(masked, axis=-1, keepdims=True))
            weights = jnp.where(allowed[None], jnp.exp(scores - highest), 0.0)
            running_sum = lax.optimization_barrier(jnp.sum(weights, axis=-1, keepdims=True))
            rounded = lax.optimization_barrier(weights.astype(jnp.bfloat16))
            mixed_output = jnp.einsum('gqk,kd->gqd', rounded.astype(jnp.float32), every_value[:, group_number].astype(jnp.float32)) / running_sum
            outputs.append(mixed_output.transpose(1, 0, 2))
        attention_result = jnp.concatenate(outputs, axis=1).reshape(TOKEN_BLOCK, QUERY_HEADS * HEAD_SIZE).astype(jnp.bfloat16)
        projected_rows = jnp.dot(attention_result, output_weight, preferred_element_type=jnp.float32)
        projected_rows = projected_rows + adapter_scale * adapter_change(attention_result, within_prompt, adapter_output_down[adapter_row], adapter_output_up[adapter_row])
        return (block_rows.astype(jnp.float32) + projected_rows).astype(jnp.bfloat16)
    residual = lax.map(attend_block, (blocks, lengths, prompt_adapter)).reshape(TOKENS, MODEL_DIM)
    normed_two = rms_scaled(residual, expert_norm_gain)
    logits = jnp.dot(normed_two, router, preferred_element_type=jnp.float32)
    squashed = jax.nn.sigmoid(jnp.take_along_axis(logits, routes, axis=1))
    mixing = squashed / lax.optimization_barrier(jnp.sum(squashed, axis=1, keepdims=True))
    devices_all = TOKENS // TOK_DEV
    per_device = routes.reshape(devices_all, TOK_DEV * TOPK)
    slots = jax.vmap(lambda flat_rows: route_slots(flat_rows, EXPERTS))(per_device).reshape(TOKENS, TOPK)
    places = (jnp.arange(TOKENS, dtype=jnp.int32) // TOK_DEV)[:, None] * CAP + slots
    slot_limit = devices_all * CAP

    def expert_step(combined, expert_id):
        buffer_rows = jnp.zeros((slot_limit, MODEL_DIM), jnp.bfloat16)
        for route_k in range(TOPK):
            target = jnp.where(routes[:, route_k] == expert_id, places[:, route_k], slot_limit)
            buffer_rows = buffer_rows.at[target].set(normed_two, mode='drop')
        gate_vals = jnp.dot(buffer_rows, expert_gate_weight[expert_id], preferred_element_type=jnp.float32)
        up_vals = jnp.dot(buffer_rows, expert_up_weight[expert_id], preferred_element_type=jnp.float32)
        hidden_vals = (jnp.maximum(gate_vals, 0.0) * up_vals).astype(jnp.bfloat16)
        answer = jnp.dot(hidden_vals, expert_down_weight[expert_id], preferred_element_type=jnp.float32).astype(jnp.bfloat16)
        for route_k in range(TOPK):
            matches = routes[:, route_k] == expert_id
            fetched = answer[jnp.minimum(places[:, route_k], slot_limit - 1)].astype(jnp.float32)
            combined = combined + jnp.where(matches[:, None], fetched * mixing[:, route_k:route_k + 1], 0.0)
        return (combined, expert_id)
    combined = lax.scan(expert_step, jnp.zeros((TOKENS, MODEL_DIM), jnp.float32), jnp.arange(EXPERTS, dtype=jnp.int32))[0]
    return (residual.astype(jnp.float32) + combined).astype(jnp.bfloat16)
```

```python
import functools

import jax
import jax.numpy as jnp
from jax import lax
from jax.experimental import pallas as pl
from jax.experimental.pallas import tpu as pltpu
from jax.sharding import PartitionSpec as P

QUERY_HEADS = 12
KEY_HEADS = 2
HEAD_SIZE = 128
QUERY_PER_KEY = 6
CAP = 40


norm_eps = 1e-06
rope_base = 1000000.0
adapter_scale = 0.5


def rms_scaled(value_tensor, norm_gain):
    widened = value_tensor.astype(jnp.float32)
    inverse = lax.rsqrt(jnp.mean(widened * widened, axis=-1, keepdims=True) + norm_eps)
    return (widened * inverse * norm_gain.astype(jnp.float32)).astype(jnp.bfloat16)


def prompt_layout(lengths_row, tok_index):
    prompt_ends = jnp.cumsum(lengths_row)
    starts = prompt_ends - lengths_row
    prompt_of = jnp.sum((tok_index[:, None] >= prompt_ends[None, :]).astype(jnp.int32), axis=1)
    within_prompt = prompt_of[:, None] == jnp.arange(lengths_row.shape[0], dtype=jnp.int32)[None, :]
    token_positions = tok_index - jnp.sum(jnp.where(within_prompt, starts[None, :], 0), axis=1)
    return (prompt_of, within_prompt, token_positions)


def apply_rotary(value_tensor, token_positions):
    half_width = value_tensor.shape[-1] // 2
    frequency = rope_base ** (
        -2.0 * jnp.arange(half_width, dtype=jnp.float32) / value_tensor.shape[-1]
    )
    angles = token_positions.astype(jnp.float32)[:, None] * frequency[None, :]
    cosine = jnp.cos(angles)[:, None, :]
    sine_part = jnp.sin(angles)[:, None, :]
    front_half = value_tensor[..., :half_width]
    back_half = value_tensor[..., half_width:]
    return jnp.concatenate(
        [front_half * cosine - back_half * sine_part, back_half * cosine + front_half * sine_part],
        axis=-1,
    )


def adapter_change(inputs, within_prompt, downs, ups):
    low_rank = jnp.einsum("nk,prk->npr", inputs, downs, preferred_element_type=jnp.float32)
    low_rank = jnp.where(within_prompt[:, :, None], low_rank, 0.0).astype(jnp.bfloat16)
    return jnp.einsum("npr,pro->no", low_rank, ups, preferred_element_type=jnp.float32)


def route_slots(flat_routes, expert_total):
    marks = (flat_routes[:, None] == jnp.arange(expert_total, dtype=jnp.int32)[None, :]).astype(
        jnp.int32
    )
    before = jnp.cumsum(marks, axis=0) - marks
    return jnp.sum(before * marks, axis=1)


def meet(peers):
    barrier = pltpu.get_barrier_semaphore()
    for peer in peers:
        pl.semaphore_signal(
            barrier, inc=1, device_id=peer, device_id_type=pl.DeviceIdType.MESH
        )
    pl.semaphore_wait(barrier, len(peers))


def remote(source, target, send_sem, recv_sem, peer):
    return pltpu.make_async_remote_copy(
        src_ref=source,
        dst_ref=target,
        send_sem=send_sem,
        recv_sem=recv_sem,
        device_id=peer,
        device_id_type=pl.DeviceIdType.MESH,
    )


def gather_kernel(
    rows,
    columns,
    proj_ref,
    out_ref,
    maps_ref,
    all_proj,
    all_out,
    all_maps,
    parts,
    chunk,
    own_sem,
    line_send,
    line_recv,
    plane_send,
    plane_recv,
    pair_send,
    pair_recv,
    part_send,
    part_recv,
    map_send,
    map_recv,
):
    row = lax.axis_index("row")
    col = lax.axis_index("col")
    chips = columns // 2
    core = lax.rem(col, 2)
    chip = col // 2
    sibling = chip * 2 + 1 - core
    square = chips == 4

    def at_row(target):
        return {"row": target, "col": col}

    def at_col(target):
        return {"row": row, "col": target}

    peers = [at_row(lax.rem(row + s, rows)) for s in range(1, rows)]
    peers += [at_col(lax.rem(col + s, columns)) for s in range(1, columns)]
    meet(peers)

    shards = (proj_ref, out_ref)
    depth = proj_ref.shape[0]
    width = proj_ref.shape[1]
    half = depth // 2

    def place(which, block_row, block_col, part=None):
        first = 0 if part is None else part * half
        size = depth if part is None else half
        if which == 0:
            return all_proj.at[
                pl.ds(pl.multiple_of(block_row * depth + first, 16), size),
                pl.ds(pl.multiple_of(block_col * width, width), width),
            ]
        return all_out.at[block_row, block_col, pl.ds(first, size)]

    pending = []

    def go(copy):
        copy.start()
        pending.append(copy)
        return copy

    part_copies = []
    for s in range(1, columns):
        target = lax.rem(col + s, columns)
        part_copies.append(
            go(
                remote(
                    maps_ref.at[target],
                    parts.at[s - 1],
                    part_send.at[s - 1],
                    part_recv.at[s - 1],
                    at_col(target),
                )
            )
        )
    line = {}

    def start_line(which):
        for s in range(1, rows):
            line[which, s] = go(
                remote(
                    shards[which],
                    place(which, row, col),
                    line_send.at[which, s - 1],
                    line_recv.at[which, s - 1],
                    at_row(lax.rem(row + s, rows)),
                )
            )

    start_line(0)
    own = []
    for which in range(2):
        own.append(
            pltpu.make_async_copy(shards[which], place(which, row, col), own_sem.at[which])
        )
        own[-1].start()

    if square:
        across = lax.rem(chip, 2)
        upward = chip // 2
        chip_x = upward * 2 + 1 - across
        chip_y = (1 - upward) * 2 + across
        chip_d = (1 - upward) * 2 + 1 - across
        senders = [chip_x, chip_y]
        targets = [chip_x, chip_y]
    else:
        targets = [lax.rem(chip + t, chips) for t in range(1, chips)]
        senders = [lax.rem(chip + chips - t, chips) for t in range(1, chips)]

    plane = {}
    pair = {}

    def to_pair(which, s, slot, source, target):
        pair[which, s, slot] = go(
            remote(
                source,
                target,
                pair_send.at[which, s, slot],
                pair_recv.at[which, s, slot],
                at_col(sibling),
            )
        )

    def spread(which, s):
        block_row = lax.rem(row + rows - s, rows)
        if s > 0:
            line[which, s].wait_recv()
            source = place(which, block_row, col)
        else:
            source = shards[which]
        for t, target in enumerate(targets):
            plane[which, s, t] = go(
                remote(
                    source,
                    place(which, block_row, col),
                    plane_send.at[which, s, t],
                    plane_recv.at[which, s, t],
                    at_col(target * 2 + core),
                )
            )
        to_pair(which, s, 0, source, place(which, block_row, col))

    def relay(which, s):
        block_row = lax.rem(row + rows - s, rows)
        for t, sender in enumerate(senders):
            plane[which, s, t].wait_recv()
            if square:
                onward = place(which, block_row, sender * 2 + core, t)
                plane[which, s, 2 + t] = go(
                    remote(
                        onward,
                        onward,
                        plane_send.at[which, s, 2 + t],
                        plane_recv.at[which, s, 2 + t],
                        at_col(targets[1 - t] * 2 + core),
                    )
                )
            here = place(which, block_row, sender * 2 + core)
            to_pair(which, s, 1 + t, here, here)

    def corner(which, s):
        if not square:
            return
        block_row = lax.rem(row + rows - s, rows)
        for t in range(2):
            plane[which, s, 2 + t].wait_recv()
        here = place(which, block_row, chip_d * 2 + core)
        to_pair(which, s, 3, here, here)

    steps = [(which, s) for which in range(2) for s in range(rows)]
    for i, step in enumerate(steps):
        spread(*step)
        if i == 0:
            total = maps_ref[col].astype(jnp.float32)
            for s in range(1, columns):
                part_copies[s - 1].wait_recv()
                total = total + parts[s - 1].astype(jnp.float32)
            chunk[...] = total.astype(jnp.bfloat16)
            map_copies = []
            for s in range(1, columns):
                map_copies.append(
                    go(
                        remote(
                            chunk,
                            all_maps.at[col],
                            map_send.at[s - 1],
                            map_recv.at[s - 1],
                            at_col(lax.rem(col + s, columns)),
                        )
                    )
                )
            mine = pltpu.make_async_copy(chunk, all_maps.at[col], own_sem.at[2])
            mine.start()
            start_line(1)
        if i >= 1:
            relay(*steps[i - 1])
        if i >= 2:
            corner(*steps[i - 2])
    relay(*steps[-1])
    corner(*steps[-2])
    corner(*steps[-1])
    for key in pair:
        pair[key].wait_recv()
    for copy in map_copies:
        copy.wait_recv()
    for copy in own:
        copy.wait()
    mine.wait()
    for copy in pending:
        copy.wait_send()


def gather_weights(projection_weight, output_weight, maps):
    rows = lax.axis_size("row")
    columns = lax.axis_size("col")
    dma = pltpu.SemaphoreType.DMA
    slots = 4 if columns == 8 else columns // 2
    anywhere = pl.BlockSpec(memory_space=pl.ANY)
    return pl.pallas_call(
        functools.partial(gather_kernel, rows, columns),
        out_shape=(
            jax.ShapeDtypeStruct(
                (projection_weight.shape[0] * rows, projection_weight.shape[1] * columns),
                jnp.bfloat16,
            ),
            jax.ShapeDtypeStruct((rows, columns) + output_weight.shape, jnp.bfloat16),
            jax.ShapeDtypeStruct(maps.shape, jnp.bfloat16),
        ),
        in_specs=[anywhere, anywhere, pl.BlockSpec(memory_space=pltpu.VMEM)],
        out_specs=(anywhere, anywhere, anywhere),
        scratch_shapes=[
            pltpu.VMEM((columns - 1,) + maps.shape[1:], jnp.bfloat16),
            pltpu.VMEM(maps.shape[1:], jnp.bfloat16),
            dma((3,)),
            dma((2, rows - 1)),
            dma((2, rows - 1)),
            dma((2, rows, slots)),
            dma((2, rows, slots)),
            dma((2, rows, slots)),
            dma((2, rows, slots)),
            dma((columns - 1,)),
            dma((columns - 1,)),
            dma((columns - 1,)),
            dma((columns - 1,)),
        ],
        compiler_params=pltpu.CompilerParams(
            collective_id=0, has_side_effects=True, vmem_limit_bytes=16 * 1024 * 1024
        ),
        name="gather_weights",
    )(projection_weight, output_weight, maps)


def share_kernel(columns, exchange, block_ref, all_ref, own_sem, send_sem, recv_sem):
    row = lax.axis_index("row")
    col = lax.axis_index("col")
    others = [lax.rem(col + s, columns) for s in range(1, columns)]
    meet([{"row": row, "col": other} for other in others])
    copies = []
    for s, other in enumerate(others):
        copies.append(
            remote(
                block_ref.at[other] if exchange else block_ref,
                all_ref.at[col],
                send_sem.at[s],
                recv_sem.at[s],
                {"row": row, "col": other},
            )
        )
        copies[-1].start()
    mine = pltpu.make_async_copy(
        block_ref.at[col] if exchange else block_ref, all_ref.at[col], own_sem
    )
    mine.start()
    mine.wait()
    for copy in copies:
        copy.wait()


def share(block, exchange, identity):
    columns = lax.axis_size("col")
    dma = pltpu.SemaphoreType.DMA
    shape = block.shape if exchange else (columns,) + block.shape
    return pl.pallas_call(
        functools.partial(share_kernel, columns, exchange),
        out_shape=jax.ShapeDtypeStruct(shape, block.dtype),
        in_specs=[pl.BlockSpec(memory_space=pl.ANY)],
        out_specs=pl.BlockSpec(memory_space=pl.ANY),
        scratch_shapes=[dma, dma((columns - 1,)), dma((columns - 1,))],
        compiler_params=pltpu.CompilerParams(
            collective_id=identity, has_side_effects=True, vmem_limit_bytes=16 * 1024 * 1024
        ),
        name="exchange" if exchange else "share",
    )(block)


def local(
    hidden_input,
    lengths,
    prompt_adapter,
    routes,
    attention_norm_gain,
    expert_norm_gain,
    projection_weight,
    output_weight,
    router,
    adapter_projection_down,
    adapter_projection_up,
    adapter_output_down,
    adapter_output_up,
    expert_gate_weight,
    expert_up_weight,
    expert_down_weight,
):
    token_rows = hidden_input.shape[0]
    model_width = hidden_input.shape[1]
    columns = lax.axis_size("col")
    row_index = lax.axis_index("row")
    col_index = lax.axis_index("col")
    lengths_row = lax.dynamic_index_in_dim(lengths, row_index, 0, keepdims=False)
    adapter_row = lax.dynamic_index_in_dim(prompt_adapter, row_index, 0, keepdims=False)
    tok_index = col_index * token_rows + jnp.arange(token_rows, dtype=jnp.int32)
    prompt_of, within_prompt, token_positions = prompt_layout(lengths_row, tok_index)
    owner_column = adapter_row // adapter_projection_down.shape[0]
    nearby_slot = adapter_row % adapter_projection_down.shape[0]
    owned_here = (owner_column == col_index)[:, None, None]

    def choose_experts(table):
        return jnp.where(owned_here, jnp.take(table, nearby_slot, axis=0).astype(jnp.float32), 0.0)

    tables = (
        adapter_projection_down,
        adapter_projection_up,
        adapter_output_down,
        adapter_output_up,
    )
    chosen = jnp.concatenate(
        [choose_experts(table).astype(jnp.bfloat16) for table in tables], axis=2
    )
    prompts, rank, map_width = chosen.shape
    splits = columns // prompts
    chosen = (
        chosen.reshape(prompts, rank, splits, map_width // splits)
        .transpose(0, 2, 1, 3)
        .reshape(columns, rank, map_width // splits)
    )
    qkv_full, out_blocks, all_maps = gather_weights(projection_weight, output_weight, chosen)
    out_full = out_blocks.transpose(0, 2, 1, 3).reshape(
        output_weight.shape[0] * lax.axis_size("row"), output_weight.shape[1] * columns
    )
    all_maps = (
        all_maps.reshape(prompts, splits, rank, map_width // splits)
        .transpose(0, 2, 1, 3)
        .reshape(prompts, rank, map_width)
    )
    cuts = []
    for table in tables:
        cuts.append((cuts[-1] if cuts else 0) + table.shape[2])
    projection_down_map, projection_up_map, output_down_map, output_up_map = jnp.split(
        all_maps, cuts[:-1], axis=2
    )
    normalized = rms_scaled(hidden_input, attention_norm_gain)
    projection_all = jnp.dot(normalized, qkv_full, preferred_element_type=jnp.float32)
    projection_all = projection_all + adapter_scale * adapter_change(
        normalized, within_prompt, projection_down_map, projection_up_map
    )
    query_slice = apply_rotary(
        projection_all[:, : QUERY_HEADS * HEAD_SIZE].reshape(token_rows, QUERY_HEADS, HEAD_SIZE),
        token_positions,
    ).astype(jnp.bfloat16)
    key_slice = apply_rotary(
        projection_all[:, QUERY_HEADS * HEAD_SIZE : (QUERY_HEADS + KEY_HEADS) * HEAD_SIZE].reshape(
            token_rows, KEY_HEADS, HEAD_SIZE
        ),
        token_positions,
    ).astype(jnp.bfloat16)
    value_slice = projection_all[:, (QUERY_HEADS + KEY_HEADS) * HEAD_SIZE :].astype(jnp.bfloat16)
    flattened_keys = key_slice.reshape(token_rows, KEY_HEADS * HEAD_SIZE)
    grouped = (
        query_slice.reshape(token_rows, KEY_HEADS, QUERY_PER_KEY, HEAD_SIZE)
        .transpose(1, 2, 0, 3)
        .reshape(KEY_HEADS, QUERY_PER_KEY * token_rows, HEAD_SIZE)
    )
    query_index = jnp.tile(tok_index, QUERY_PER_KEY)
    query_prompt = jnp.tile(prompt_of, QUERY_PER_KEY)
    shared = share(jnp.concatenate([flattened_keys, value_slice], axis=1), False, 1)
    shared = shared.reshape(columns * token_rows, 2 * KEY_HEADS * HEAD_SIZE)
    segments = (shared[:, : KEY_HEADS * HEAD_SIZE], shared[:, KEY_HEADS * HEAD_SIZE :])
    best_experts = jnp.full((KEY_HEADS, QUERY_PER_KEY * token_rows), -1e30, jnp.float32)
    segment_length = segments[0].shape[0]
    key_lines = segments[0].reshape(segment_length, KEY_HEADS, HEAD_SIZE).transpose(1, 0, 2)
    value_lines = segments[1].reshape(segment_length, KEY_HEADS, HEAD_SIZE).transpose(1, 0, 2)
    key_index = jnp.arange(segment_length, dtype=jnp.int32)
    key_prompt = prompt_layout(lengths_row, key_index)[0]
    allowed = (key_prompt[None, :] == query_prompt[:, None]) & (
        key_index[None, :] <= query_index[:, None]
    )
    scores = jnp.einsum(
        "hqd,hkd->hqk", grouped, key_lines, preferred_element_type=jnp.float32
    ) * HEAD_SIZE ** (-0.5)
    masked = jnp.where(allowed[None], scores, -1e30)
    fresh = jnp.maximum(best_experts, jnp.max(masked, axis=-1))
    weights = jnp.where(allowed[None], jnp.exp(scores - fresh[..., None]), 0.0)
    running_new = jnp.sum(weights, axis=-1)
    accum_new = jnp.einsum(
        "hqk,hkd->hqd",
        weights.astype(jnp.bfloat16),
        value_lines,
        preferred_element_type=jnp.float32,
    )
    mixed_output = accum_new / running_new[..., None]
    attention_result = (
        mixed_output.reshape(KEY_HEADS, QUERY_PER_KEY, token_rows, HEAD_SIZE)
        .transpose(2, 0, 1, 3)
        .reshape(token_rows, QUERY_HEADS * HEAD_SIZE)
        .astype(jnp.bfloat16)
    )
    projected_rows = jnp.dot(attention_result, out_full, preferred_element_type=jnp.float32)
    projected_rows = projected_rows + adapter_scale * adapter_change(
        attention_result, within_prompt, output_down_map, output_up_map
    )
    residual = (hidden_input.astype(jnp.float32) + projected_rows).astype(jnp.bfloat16)
    normed_two = rms_scaled(residual, expert_norm_gain)
    logits = jnp.dot(normed_two, router, preferred_element_type=jnp.float32)
    squashed = jax.nn.sigmoid(jnp.take_along_axis(logits, routes, axis=1))
    mixing = squashed / jnp.sum(squashed, axis=1, keepdims=True)
    expert_total = router.shape[1]
    local_experts = expert_gate_weight.shape[0]
    flat_routes = routes.reshape(-1)
    slots = route_slots(flat_routes, expert_total)
    spots = (flat_routes * CAP + slots).reshape(routes.shape)
    spot_index = jnp.arange(expert_total * CAP, dtype=jnp.int32)
    marked = spots[:, :, None] == spot_index[None, None, :]
    dispatch = jnp.any(marked, axis=1).astype(jnp.bfloat16)
    sending = jnp.einsum(
        "tj,td->jd", dispatch, normed_two, preferred_element_type=jnp.float32
    ).astype(jnp.bfloat16)
    sending = sending.reshape(columns, local_experts * CAP, model_width)
    arrived = share(sending, True, 2).reshape(columns, local_experts, CAP, model_width)
    gate_vals = jnp.einsum(
        "sjcd,jdf->sjcf", arrived, expert_gate_weight, preferred_element_type=jnp.float32
    )
    up_vals = jnp.einsum(
        "sjcd,jdf->sjcf", arrived, expert_up_weight, preferred_element_type=jnp.float32
    )
    hidden_vals = (jnp.maximum(gate_vals, 0.0) * up_vals).astype(jnp.bfloat16)
    answered = jnp.einsum(
        "sjcf,jfd->sjcd", hidden_vals, expert_down_weight, preferred_element_type=jnp.float32
    ).astype(jnp.bfloat16)
    returned = share(
        answered.reshape(columns, local_experts * CAP, model_width), True, 3
    ).reshape(expert_total * CAP, model_width)
    mix = jnp.sum(jnp.where(marked, mixing[:, :, None], 0.0), axis=1)
    mix_high = mix.astype(jnp.bfloat16)
    mix_low = (mix - mix_high.astype(jnp.float32)).astype(jnp.bfloat16)
    combined = jnp.dot(mix_high, returned, preferred_element_type=jnp.float32) + jnp.dot(
        mix_low, returned, preferred_element_type=jnp.float32
    )
    return (residual.astype(jnp.float32) + combined).astype(jnp.bfloat16)


def solution(mesh):
    placed = (
        P(("row", "col"), None),
        P(),
        P(),
        P(("row", "col"), None),
        P(),
        P(),
        P("row", "col"),
        P("row", "col"),
        P(),
        P("col", None, None),
        P("col", None, None),
        P("col", None, None),
        P("col", None, None),
        P("col", None, None),
        P("col", None, None),
        P("col", None, None),
    )
    return jax.shard_map(
        local, mesh=mesh, in_specs=placed, out_specs=P(("row", "col"), None), check_vma=False
    )
```

```python
import functools

import jax
import jax.numpy as jnp
from jax import lax
from jax.experimental import pallas as pl
from jax.experimental.pallas import tpu as pltpu
from jax.sharding import PartitionSpec as P

QUERY_HEADS = 12
KEY_HEADS = 2
HEAD_SIZE = 128
QUERY_PER_KEY = 6
CAP = 40


norm_eps = 1e-06
rope_base = 1000000.0
adapter_scale = 0.5


def rms_scaled(value_tensor, norm_gain):
    widened = value_tensor.astype(jnp.float32)
    inverse = lax.rsqrt(jnp.mean(widened * widened, axis=-1, keepdims=True) + norm_eps)
    return (widened * inverse * norm_gain.astype(jnp.float32)).astype(jnp.bfloat16)


def prompt_layout(lengths_row, tok_index):
    prompt_ends = jnp.cumsum(lengths_row)
    starts = prompt_ends - lengths_row
    prompt_of = jnp.sum((tok_index[:, None] >= prompt_ends[None, :]).astype(jnp.int32), axis=1)
    within_prompt = prompt_of[:, None] == jnp.arange(lengths_row.shape[0], dtype=jnp.int32)[None, :]
    token_positions = tok_index - jnp.sum(jnp.where(within_prompt, starts[None, :], 0), axis=1)
    return (prompt_of, within_prompt, token_positions)


def apply_rotary(value_tensor, token_positions):
    half_width = value_tensor.shape[-1] // 2
    frequency = rope_base ** (
        -2.0 * jnp.arange(half_width, dtype=jnp.float32) / value_tensor.shape[-1]
    )
    angles = token_positions.astype(jnp.float32)[:, None] * frequency[None, :]
    cosine = jnp.cos(angles)[:, None, :]
    sine_part = jnp.sin(angles)[:, None, :]
    front_half = value_tensor[..., :half_width]
    back_half = value_tensor[..., half_width:]
    return jnp.concatenate(
        [front_half * cosine - back_half * sine_part, back_half * cosine + front_half * sine_part],
        axis=-1,
    )


def adapter_change(inputs, within_prompt, downs, ups):
    low_rank = jnp.einsum("nk,prk->npr", inputs, downs, preferred_element_type=jnp.float32)
    low_rank = jnp.where(within_prompt[:, :, None], low_rank, 0.0).astype(jnp.bfloat16)
    return jnp.einsum("npr,pro->no", low_rank, ups, preferred_element_type=jnp.float32)


def route_slots(flat_routes, expert_total):
    marks = (flat_routes[:, None] == jnp.arange(expert_total, dtype=jnp.int32)[None, :]).astype(
        jnp.int32
    )
    before = jnp.cumsum(marks, axis=0) - marks
    return jnp.sum(before * marks, axis=1)


def meet(peers):
    barrier = pltpu.get_barrier_semaphore()
    for peer in peers:
        pl.semaphore_signal(
            barrier, inc=1, device_id=peer, device_id_type=pl.DeviceIdType.MESH
        )
    pl.semaphore_wait(barrier, len(peers))


def remote(source, target, send_sem, recv_sem, peer):
    return pltpu.make_async_remote_copy(
        src_ref=source,
        dst_ref=target,
        send_sem=send_sem,
        recv_sem=recv_sem,
        device_id=peer,
        device_id_type=pl.DeviceIdType.MESH,
    )


def gather_kernel(
    rows,
    columns,
    proj_ref,
    out_ref,
    maps_ref,
    all_proj,
    all_out,
    all_maps,
    parts,
    chunk,
    own_sem,
    line_send,
    line_recv,
    plane_send,
    plane_recv,
    pair_send,
    pair_recv,
    part_send,
    part_recv,
    map_send,
    map_recv,
):
    row = lax.axis_index("row")
    col = lax.axis_index("col")
    chips = columns // 2
    core = lax.rem(col, 2)
    chip = col // 2
    sibling = chip * 2 + 1 - core
    square = chips == 4

    def at_row(target):
        return {"row": target, "col": col}

    def at_col(target):
        return {"row": row, "col": target}

    peers = [at_row(lax.rem(row + s, rows)) for s in range(1, rows)]
    peers += [at_col(lax.rem(col + s, columns)) for s in range(1, columns)]
    meet(peers)

    shards = (proj_ref, out_ref)
    depth = proj_ref.shape[0]
    width = proj_ref.shape[1]
    out_depth, out_width = out_ref.shape

    def place(which, block_row, block_col, part=None):
        tall = depth if which == 0 else out_depth
        first = 0 if part is None else part * (tall // 2)
        size = tall if part is None else tall // 2
        if which == 0:
            return all_proj.at[
                pl.ds(pl.multiple_of(block_row * depth + first, 16), size),
                pl.ds(pl.multiple_of(block_col * width, width), width),
            ]
        return all_out.at[
            pl.ds(pl.multiple_of(block_row * out_depth + first, 16), size),
            pl.ds(pl.multiple_of(block_col * out_width, 128), out_width),
        ]

    pending = []

    def go(copy):
        copy.start()
        pending.append(copy)
        return copy

    part_copies = []
    for s in range(1, columns):
        target = lax.rem(col + s, columns)
        part_copies.append(
            go(
                remote(
                    maps_ref.at[target],
                    parts.at[s - 1],
                    part_send.at[s - 1],
                    part_recv.at[s - 1],
                    at_col(target),
                )
            )
        )
    line = {}

    def start_line(which):
        for s in range(1, rows):
            line[which, s] = go(
                remote(
                    shards[which],
                    place(which, row, col),
                    line_send.at[which, s - 1],
                    line_recv.at[which, s - 1],
                    at_row(lax.rem(row + s, rows)),
                )
            )

    start_line(0)
    own = []
    for which in range(2):
        own.append(
            pltpu.make_async_copy(shards[which], place(which, row, col), own_sem.at[which])
        )
        own[-1].start()

    if square:
        across = lax.rem(chip, 2)
        upward = chip // 2
        chip_x = upward * 2 + 1 - across
        chip_y = (1 - upward) * 2 + across
        chip_d = (1 - upward) * 2 + 1 - across
        senders = [chip_x, chip_y]
        targets = [chip_x, chip_y]
    else:
        targets = [lax.rem(chip + t, chips) for t in range(1, chips)]
        senders = [lax.rem(chip + chips - t, chips) for t in range(1, chips)]

    plane = {}
    pair = {}

    def to_pair(which, s, slot, source, target):
        pair[which, s, slot] = go(
            remote(
                source,
                target,
                pair_send.at[which, s, slot],
                pair_recv.at[which, s, slot],
                at_col(sibling),
            )
        )

    def spread(which, s):
        block_row = lax.rem(row + rows - s, rows)
        if s > 0:
            line[which, s].wait_recv()
            source = place(which, block_row, col)
        else:
            source = shards[which]
        for t, target in enumerate(targets):
            plane[which, s, t] = go(
                remote(
                    source,
                    place(which, block_row, col),
                    plane_send.at[which, s, t],
                    plane_recv.at[which, s, t],
                    at_col(target * 2 + core),
                )
            )
        to_pair(which, s, 0, source, place(which, block_row, col))

    def relay(which, s):
        block_row = lax.rem(row + rows - s, rows)
        for t, sender in enumerate(senders):
            plane[which, s, t].wait_recv()
            if square:
                onward = place(which, block_row, sender * 2 + core, t)
                plane[which, s, 2 + t] = go(
                    remote(
                        onward,
                        onward,
                        plane_send.at[which, s, 2 + t],
                        plane_recv.at[which, s, 2 + t],
                        at_col(targets[1 - t] * 2 + core),
                    )
                )
            here = place(which, block_row, sender * 2 + core)
            to_pair(which, s, 1 + t, here, here)

    def corner(which, s):
        if not square:
            return
        block_row = lax.rem(row + rows - s, rows)
        for t in range(2):
            plane[which, s, 2 + t].wait_recv()
        here = place(which, block_row, chip_d * 2 + core)
        to_pair(which, s, 3, here, here)

    steps = [(which, s) for which in range(2) for s in range(rows)]
    for i, step in enumerate(steps):
        spread(*step)
        if i == 0:
            total = maps_ref[col].astype(jnp.float32)
            for s in range(1, columns):
                part_copies[s - 1].wait_recv()
                total = total + parts[s - 1].astype(jnp.float32)
            chunk[...] = total.astype(jnp.bfloat16)
            map_copies = []
            for s in range(1, columns):
                map_copies.append(
                    go(
                        remote(
                            chunk,
                            all_maps.at[col],
                            map_send.at[s - 1],
                            map_recv.at[s - 1],
                            at_col(lax.rem(col + s, columns)),
                        )
                    )
                )
            mine = pltpu.make_async_copy(chunk, all_maps.at[col], own_sem.at[2])
            mine.start()
            start_line(1)
        if i >= 1:
            relay(*steps[i - 1])
        if i >= 2:
            corner(*steps[i - 2])
    relay(*steps[-1])
    corner(*steps[-2])
    corner(*steps[-1])
    for key in pair:
        pair[key].wait_recv()
    for copy in map_copies:
        copy.wait_recv()
    for copy in own:
        copy.wait()
    mine.wait()
    for copy in pending:
        copy.wait_send()


def gather_weights(projection_weight, output_weight, maps):
    rows = lax.axis_size("row")
    columns = lax.axis_size("col")
    dma = pltpu.SemaphoreType.DMA
    slots = 4 if columns == 8 else columns // 2
    anywhere = pl.BlockSpec(memory_space=pl.ANY)
    return pl.pallas_call(
        functools.partial(gather_kernel, rows, columns),
        out_shape=(
            jax.ShapeDtypeStruct(
                (projection_weight.shape[0] * rows, projection_weight.shape[1] * columns),
                jnp.bfloat16,
            ),
            jax.ShapeDtypeStruct(
                (output_weight.shape[0] * rows, output_weight.shape[1] * columns), jnp.bfloat16
            ),
            jax.ShapeDtypeStruct(maps.shape, jnp.bfloat16),
        ),
        in_specs=[anywhere, anywhere, pl.BlockSpec(memory_space=pltpu.VMEM)],
        out_specs=(anywhere, anywhere, anywhere),
        scratch_shapes=[
            pltpu.VMEM((columns - 1,) + maps.shape[1:], jnp.bfloat16),
            pltpu.VMEM(maps.shape[1:], jnp.bfloat16),
            dma((3,)),
            dma((2, rows - 1)),
            dma((2, rows - 1)),
            dma((2, rows, slots)),
            dma((2, rows, slots)),
            dma((2, rows, slots)),
            dma((2, rows, slots)),
            dma((columns - 1,)),
            dma((columns - 1,)),
            dma((columns - 1,)),
            dma((columns - 1,)),
        ],
        compiler_params=pltpu.CompilerParams(
            collective_id=0, has_side_effects=True, vmem_limit_bytes=16 * 1024 * 1024
        ),
        name="gather_weights",
    )(projection_weight, output_weight, maps)


def share_kernel(columns, exchange, block_ref, all_ref, own_sem, send_sem, recv_sem):
    row = lax.axis_index("row")
    col = lax.axis_index("col")
    others = [lax.rem(col + s, columns) for s in range(1, columns)]
    meet([{"row": row, "col": other} for other in others])
    copies = []
    for s, other in enumerate(others):
        copies.append(
            remote(
                block_ref.at[other] if exchange else block_ref,
                all_ref.at[col],
                send_sem.at[s],
                recv_sem.at[s],
                {"row": row, "col": other},
            )
        )
        copies[-1].start()
    mine = pltpu.make_async_copy(
        block_ref.at[col] if exchange else block_ref, all_ref.at[col], own_sem
    )
    mine.start()
    mine.wait()
    for copy in copies:
        copy.wait()


def share(block, exchange, identity):
    columns = lax.axis_size("col")
    dma = pltpu.SemaphoreType.DMA
    shape = block.shape if exchange else (columns,) + block.shape
    return pl.pallas_call(
        functools.partial(share_kernel, columns, exchange),
        out_shape=jax.ShapeDtypeStruct(shape, block.dtype),
        in_specs=[pl.BlockSpec(memory_space=pl.ANY)],
        out_specs=pl.BlockSpec(memory_space=pl.ANY),
        scratch_shapes=[dma, dma((columns - 1,)), dma((columns - 1,))],
        compiler_params=pltpu.CompilerParams(
            collective_id=identity, has_side_effects=True, vmem_limit_bytes=16 * 1024 * 1024
        ),
        name="exchange" if exchange else "share",
    )(block)


def experts_kernel(
    columns,
    sending_ref,
    gate_ref,
    up_ref,
    down_ref,
    all_ref,
    gate,
    up,
    down,
    arrived,
    answer,
    load_sem,
    own_sem,
    send_sem,
    recv_sem,
    back_send,
    back_recv,
):
    row = lax.axis_index("row")
    col = lax.axis_index("col")
    chips = columns // 2
    core = lax.rem(col, 2)
    chip = col // 2
    meet([{"row": row, "col": lax.rem(col + s, columns)} for s in range(1, columns)])
    loads = [
        pltpu.make_async_copy(gate_ref, gate, load_sem.at[0]),
        pltpu.make_async_copy(up_ref, up, load_sem.at[1]),
        pltpu.make_async_copy(down_ref, down, load_sem.at[2]),
    ]
    for load in loads:
        load.start()
    if chips == 4:
        across = lax.rem(chip, 2)
        upward = chip // 2
        targets = [
            chip,
            upward * 2 + 1 - across,
            (1 - upward) * 2 + across,
            (1 - upward) * 2 + 1 - across,
        ]
        sources = targets
    else:
        targets = [lax.rem(chip + t, chips) for t in range(chips)]
        sources = [lax.rem(chip + chips - t, chips) for t in range(chips)]
    rows = sending_ref.shape[1]
    cap = rows // gate_ref.shape[0]

    def outward(g, other):
        target = targets[g] * 2 + other
        return remote(
            sending_ref.at[target],
            arrived.at[2 * g + core],
            send_sem.at[2 * g + other],
            recv_sem.at[2 * g + core],
            {"row": row, "col": target},
        )

    def inward(g, other):
        return remote(
            sending_ref.at[col],
            arrived.at[2 * g + other],
            send_sem.at[2 * g + other],
            recv_sem.at[2 * g + other],
            {"row": row, "col": targets[g] * 2 + other},
        )

    def back(g, other):
        return remote(
            answer.at[2 * g + other],
            all_ref.at[col],
            back_send.at[2 * g + other],
            back_recv.at[2 * g + core],
            {"row": row, "col": sources[g] * 2 + other},
        )

    def back_in(g, other):
        return remote(
            answer.at[2 * g + other],
            all_ref.at[targets[g] * 2 + other],
            back_send.at[2 * g + other],
            back_recv.at[2 * g + other],
            {"row": row, "col": targets[g] * 2 + other},
        )

    def members(g):
        return [1 - core] if g == 0 else [0, 1]

    def work(g):
        held = jnp.concatenate([arrived[2 * g], arrived[2 * g + 1]], axis=0)
        spot = lax.broadcasted_iota(jnp.int32, (2 * rows, 1), 0)
        spot = jnp.where(spot >= rows, spot - rows, spot)
        total = None
        for j in range(gate.shape[0]):
            gate_vals = jnp.dot(held, gate[j], preferred_element_type=jnp.float32)
            up_vals = jnp.dot(held, up[j], preferred_element_type=jnp.float32)
            mine = (spot >= j * cap) & (spot < (j + 1) * cap)
            hidden = jnp.where(mine, jnp.maximum(gate_vals, 0.0) * up_vals, 0.0)
            part = jnp.dot(
                hidden.astype(jnp.bfloat16), down[j], preferred_element_type=jnp.float32
            )
            total = part if total is None else total + part
        total = total.astype(jnp.bfloat16)
        answer[2 * g] = total[:rows]
        answer[2 * g + 1] = total[rows:]

    first = min(chips, 3)
    sent = []
    for g in list(range(1, first)) + [0]:
        for other in members(g):
            sent.append(outward(g, other))
            sent[-1].start()
    mine = pltpu.make_async_copy(sending_ref.at[col], arrived.at[core], own_sem.at[0])
    mine.start()
    for load in loads:
        load.wait()
    mine.wait()
    for g in range(chips):
        for other in members(g):
            inward(g, other).wait_recv()
        work(g)
        if g == 0:
            for late in range(first, chips):
                for other in members(late):
                    sent.append(outward(late, other))
                    sent[-1].start()
            kept = pltpu.make_async_copy(answer.at[core], all_ref.at[col], own_sem.at[1])
            kept.start()
        for other in members(g):
            sent.append(back(g, other))
            sent[-1].start()
    for g in range(chips):
        for other in members(g):
            back_in(g, other).wait_recv()
    kept.wait()
    for copy in sent:
        copy.wait_send()


def run_experts(sending, gate, up, down):
    columns = lax.axis_size("col")
    dma = pltpu.SemaphoreType.DMA
    anywhere = pl.BlockSpec(memory_space=pl.ANY)
    return pl.pallas_call(
        functools.partial(experts_kernel, columns),
        out_shape=jax.ShapeDtypeStruct(sending.shape, jnp.bfloat16),
        in_specs=[pl.BlockSpec(memory_space=pltpu.VMEM), anywhere, anywhere, anywhere],
        out_specs=anywhere,
        scratch_shapes=[
            pltpu.VMEM(gate.shape, jnp.bfloat16),
            pltpu.VMEM(up.shape, jnp.bfloat16),
            pltpu.VMEM(down.shape, jnp.bfloat16),
            pltpu.VMEM(sending.shape, jnp.bfloat16),
            pltpu.VMEM(sending.shape, jnp.bfloat16),
            dma((3,)),
            dma((2,)),
            dma((columns,)),
            dma((columns,)),
            dma((columns,)),
            dma((columns,)),
        ],
        compiler_params=pltpu.CompilerParams(
            collective_id=2, has_side_effects=True, vmem_limit_bytes=40 * 1024 * 1024
        ),
        name="run_experts",
    )(sending, gate, up, down)


def local(
    hidden_input,
    lengths,
    prompt_adapter,
    routes,
    attention_norm_gain,
    expert_norm_gain,
    projection_weight,
    output_weight,
    router,
    adapter_projection_down,
    adapter_projection_up,
    adapter_output_down,
    adapter_output_up,
    expert_gate_weight,
    expert_up_weight,
    expert_down_weight,
):
    token_rows = hidden_input.shape[0]
    model_width = hidden_input.shape[1]
    columns = lax.axis_size("col")
    row_index = lax.axis_index("row")
    col_index = lax.axis_index("col")
    lengths_row = lax.dynamic_index_in_dim(lengths, row_index, 0, keepdims=False)
    adapter_row = lax.dynamic_index_in_dim(prompt_adapter, row_index, 0, keepdims=False)
    tok_index = col_index * token_rows + jnp.arange(token_rows, dtype=jnp.int32)
    prompt_of, within_prompt, token_positions = prompt_layout(lengths_row, tok_index)
    adapter_count = adapter_projection_down.shape[0]

    def choose_experts(table):
        return sum(
            jnp.where(
                (adapter_row == col_index * adapter_count + a)[:, None, None],
                table[a][None].astype(jnp.float32),
                0.0,
            )
            for a in range(adapter_count)
        )

    tables = (
        adapter_projection_down,
        adapter_projection_up,
        adapter_output_down,
        adapter_output_up,
    )
    chosen = jnp.concatenate(
        [choose_experts(table).astype(jnp.bfloat16) for table in tables], axis=2
    )
    prompts, rank, map_width = chosen.shape
    splits = columns // prompts
    chosen = (
        chosen.reshape(prompts, rank, splits, map_width // splits)
        .transpose(0, 2, 1, 3)
        .reshape(columns, rank, map_width // splits)
    )
    out_depth, out_width = output_weight.shape
    paired = out_width == 192
    if paired:
        side = output_weight[:, 128:]
        packed = jnp.concatenate(
            [
                output_weight[:, :128],
                jnp.concatenate([side[: out_depth // 2], side[out_depth // 2 :]], axis=1),
            ],
            axis=0,
        )
    else:
        packed = jnp.pad(output_weight, ((0, 0), (0, -out_width % 128)))
    qkv_full, out_packed, all_maps = gather_weights(projection_weight, packed, chosen)
    all_maps = (
        all_maps.reshape(prompts, splits, rank, map_width // splits)
        .transpose(0, 2, 1, 3)
        .reshape(prompts, rank, map_width)
    )
    cuts = []
    for table in tables:
        cuts.append((cuts[-1] if cuts else 0) + table.shape[2])
    projection_down_map, projection_up_map, output_down_map, output_up_map = jnp.split(
        all_maps, cuts[:-1], axis=2
    )
    normalized = rms_scaled(hidden_input, attention_norm_gain)
    projection_all = jnp.dot(normalized, qkv_full, preferred_element_type=jnp.float32)
    projection_all = projection_all + adapter_scale * adapter_change(
        normalized, within_prompt, projection_down_map, projection_up_map
    )
    query_slice = apply_rotary(
        projection_all[:, : QUERY_HEADS * HEAD_SIZE].reshape(token_rows, QUERY_HEADS, HEAD_SIZE),
        token_positions,
    ).astype(jnp.bfloat16)
    key_slice = apply_rotary(
        projection_all[:, QUERY_HEADS * HEAD_SIZE : (QUERY_HEADS + KEY_HEADS) * HEAD_SIZE].reshape(
            token_rows, KEY_HEADS, HEAD_SIZE
        ),
        token_positions,
    ).astype(jnp.bfloat16)
    value_slice = projection_all[:, (QUERY_HEADS + KEY_HEADS) * HEAD_SIZE :].astype(jnp.bfloat16)
    flattened_keys = key_slice.reshape(token_rows, KEY_HEADS * HEAD_SIZE)
    grouped = (
        query_slice.reshape(token_rows, KEY_HEADS, QUERY_PER_KEY, HEAD_SIZE)
        .transpose(1, 2, 0, 3)
        .reshape(KEY_HEADS, QUERY_PER_KEY * token_rows, HEAD_SIZE)
    )
    query_index = jnp.tile(tok_index, QUERY_PER_KEY)
    query_prompt = jnp.tile(prompt_of, QUERY_PER_KEY)
    shared = share(jnp.concatenate([flattened_keys, value_slice], axis=1), False, 1)
    shared = shared.reshape(columns * token_rows, 2 * KEY_HEADS * HEAD_SIZE)
    segments = (shared[:, : KEY_HEADS * HEAD_SIZE], shared[:, KEY_HEADS * HEAD_SIZE :])
    best_experts = jnp.full((KEY_HEADS, QUERY_PER_KEY * token_rows), -1e30, jnp.float32)
    segment_length = segments[0].shape[0]
    key_lines = segments[0].reshape(segment_length, KEY_HEADS, HEAD_SIZE).transpose(1, 0, 2)
    value_lines = segments[1].reshape(segment_length, KEY_HEADS, HEAD_SIZE).transpose(1, 0, 2)
    key_index = jnp.arange(segment_length, dtype=jnp.int32)
    key_prompt = prompt_layout(lengths_row, key_index)[0]
    allowed = (key_prompt[None, :] == query_prompt[:, None]) & (
        key_index[None, :] <= query_index[:, None]
    )
    scores = jnp.einsum(
        "hqd,hkd->hqk", grouped, key_lines, preferred_element_type=jnp.float32
    ) * HEAD_SIZE ** (-0.5)
    masked = jnp.where(allowed[None], scores, -1e30)
    fresh = jnp.maximum(best_experts, jnp.max(masked, axis=-1))
    weights = jnp.where(allowed[None], jnp.exp(scores - fresh[..., None]), 0.0)
    running_new = jnp.sum(weights, axis=-1)
    accum_new = jnp.einsum(
        "hqk,hkd->hqd",
        weights.astype(jnp.bfloat16),
        value_lines,
        preferred_element_type=jnp.float32,
    )
    mixed_output = accum_new / running_new[..., None]
    attention_result = (
        mixed_output.reshape(KEY_HEADS, QUERY_PER_KEY, token_rows, HEAD_SIZE)
        .transpose(2, 0, 1, 3)
        .reshape(token_rows, QUERY_HEADS * HEAD_SIZE)
        .astype(jnp.bfloat16)
    )
    row_count = lax.axis_size("row")
    if paired:
        stacked = out_packed.reshape(row_count, packed.shape[0], columns * 128)
        attended_parts = attention_result.reshape(token_rows, row_count, out_depth)
        front = jnp.einsum(
            "trk,rkn->tn",
            attended_parts,
            stacked[:, :out_depth],
            preferred_element_type=jnp.float32,
        ).reshape(token_rows, columns, 128)
        halves = [
            jnp.einsum(
                "trk,rkn->tn",
                attended_parts[:, :, h * (out_depth // 2) : (h + 1) * (out_depth // 2)],
                stacked[:, out_depth:],
                preferred_element_type=jnp.float32,
            ).reshape(token_rows, columns, 128)[:, :, h * 64 : (h + 1) * 64]
            for h in range(2)
        ]
        projected_rows = jnp.concatenate([front, halves[0] + halves[1]], axis=2)
    else:
        projected_rows = jnp.dot(
            attention_result, out_packed, preferred_element_type=jnp.float32
        ).reshape(token_rows, columns, packed.shape[1])[:, :, :out_width]
    projected_rows = projected_rows.reshape(token_rows, model_width)
    projected_rows = projected_rows + adapter_scale * adapter_change(
        attention_result, within_prompt, output_down_map, output_up_map
    )
    residual = (hidden_input.astype(jnp.float32) + projected_rows).astype(jnp.bfloat16)
    normed_two = rms_scaled(residual, expert_norm_gain)
    logits = jnp.dot(normed_two, router, preferred_element_type=jnp.float32)
    squashed = jax.nn.sigmoid(
        jnp.sum(
            jnp.where(
                routes[:, :, None] == jnp.arange(router.shape[1], dtype=jnp.int32)[None, None, :],
                logits[:, None, :],
                0.0,
            ),
            axis=2,
        )
    )
    mixing = squashed / jnp.sum(squashed, axis=1, keepdims=True)
    expert_total = router.shape[1]
    local_experts = expert_gate_weight.shape[0]
    flat_routes = routes.reshape(-1)
    slots = route_slots(flat_routes, expert_total)
    spots = (flat_routes * CAP + slots).reshape(routes.shape)
    spot_index = jnp.arange(expert_total * CAP, dtype=jnp.int32)
    marked = spots[:, :, None] == spot_index[None, None, :]
    dispatch = jnp.any(marked, axis=1).astype(jnp.bfloat16)
    sending = jnp.einsum(
        "tj,td->jd", dispatch, normed_two, preferred_element_type=jnp.float32
    ).astype(jnp.bfloat16)
    sending = sending.reshape(columns, local_experts * CAP, model_width)
    returned = run_experts(
        sending, expert_gate_weight, expert_up_weight, expert_down_weight
    ).reshape(expert_total * CAP, model_width)
    mix = jnp.sum(jnp.where(marked, mixing[:, :, None], 0.0), axis=1)
    mix_high = mix.astype(jnp.bfloat16)
    mix_low = (mix - mix_high.astype(jnp.float32)).astype(jnp.bfloat16)
    combined = jnp.dot(mix_high, returned, preferred_element_type=jnp.float32) + jnp.dot(
        mix_low, returned, preferred_element_type=jnp.float32
    )
    return (residual.astype(jnp.float32) + combined).astype(jnp.bfloat16)


def solution(mesh):
    placed = (
        P(("row", "col"), None),
        P(),
        P(),
        P(("row", "col"), None),
        P(),
        P(),
        P("row", "col"),
        P("row", "col"),
        P(),
        P("col", None, None),
        P("col", None, None),
        P("col", None, None),
        P("col", None, None),
        P("col", None, None),
        P("col", None, None),
        P("col", None, None),
    )
    return jax.shard_map(
        local, mesh=mesh, in_specs=placed, out_specs=P(("row", "col"), None), check_vma=False
    )
```

```python
import functools

import jax
import jax.numpy as jnp
from jax import lax
from jax.experimental import pallas as pl
from jax.experimental.pallas import tpu as pltpu
from jax.sharding import PartitionSpec as P

QUERY_HEADS = 12
KEY_HEADS = 2
HEAD_SIZE = 128
QUERY_PER_KEY = 6
CAP = 40


norm_eps = 1e-06
rope_base = 1000000.0
adapter_scale = 0.5


def rms_scaled(value_tensor, norm_gain):
    widened = value_tensor.astype(jnp.float32)
    inverse = lax.rsqrt(jnp.mean(widened * widened, axis=-1, keepdims=True) + norm_eps)
    return (widened * inverse * norm_gain.astype(jnp.float32)).astype(jnp.bfloat16)


def prompt_layout(lengths_row, tok_index):
    prompt_ends = jnp.cumsum(lengths_row)
    starts = prompt_ends - lengths_row
    prompt_of = jnp.sum((tok_index[:, None] >= prompt_ends[None, :]).astype(jnp.int32), axis=1)
    within_prompt = prompt_of[:, None] == jnp.arange(lengths_row.shape[0], dtype=jnp.int32)[None, :]
    token_positions = tok_index - jnp.sum(jnp.where(within_prompt, starts[None, :], 0), axis=1)
    return (prompt_of, within_prompt, token_positions)


def apply_rotary(value_tensor, token_positions):
    half_width = value_tensor.shape[-1] // 2
    frequency = rope_base ** (
        -2.0 * jnp.arange(half_width, dtype=jnp.float32) / value_tensor.shape[-1]
    )
    angles = token_positions.astype(jnp.float32)[:, None] * frequency[None, :]
    cosine = jnp.cos(angles)[:, None, :]
    sine_part = jnp.sin(angles)[:, None, :]
    front_half = value_tensor[..., :half_width]
    back_half = value_tensor[..., half_width:]
    return jnp.concatenate(
        [front_half * cosine - back_half * sine_part, back_half * cosine + front_half * sine_part],
        axis=-1,
    )


def adapter_change(inputs, within_prompt, downs, ups):
    low_rank = jnp.einsum("nk,prk->npr", inputs, downs, preferred_element_type=jnp.float32)
    low_rank = jnp.where(within_prompt[:, :, None], low_rank, 0.0).astype(jnp.bfloat16)
    return jnp.einsum("npr,pro->no", low_rank, ups, preferred_element_type=jnp.float32)


def route_slots(flat_routes, expert_total):
    marks = (flat_routes[:, None] == jnp.arange(expert_total, dtype=jnp.int32)[None, :]).astype(
        jnp.int32
    )
    before = jnp.cumsum(marks, axis=0) - marks
    return jnp.sum(before * marks, axis=1)


def meet(peers):
    barrier = pltpu.get_barrier_semaphore()
    for peer in peers:
        pl.semaphore_signal(
            barrier, inc=1, device_id=peer, device_id_type=pl.DeviceIdType.MESH
        )
    pl.semaphore_wait(barrier, len(peers))


def remote(source, target, send_sem, recv_sem, peer):
    return pltpu.make_async_remote_copy(
        src_ref=source,
        dst_ref=target,
        send_sem=send_sem,
        recv_sem=recv_sem,
        device_id=peer,
        device_id_type=pl.DeviceIdType.MESH,
    )


def gather_kernel(
    rows,
    columns,
    proj_ref,
    out_ref,
    maps_ref,
    all_proj,
    all_out,
    all_maps,
    parts,
    chunk,
    own_sem,
    line_send,
    line_recv,
    plane_send,
    plane_recv,
    pair_send,
    pair_recv,
    part_send,
    part_recv,
    map_send,
    map_recv,
):
    row = lax.axis_index("row")
    col = lax.axis_index("col")
    chips = columns // 2
    core = lax.rem(col, 2)
    chip = col // 2
    sibling = chip * 2 + 1 - core
    square = chips == 4

    def at_row(target):
        return {"row": target, "col": col}

    def at_col(target):
        return {"row": row, "col": target}

    peers = [at_row(lax.rem(row + s, rows)) for s in range(1, rows)]
    peers += [at_col(lax.rem(col + s, columns)) for s in range(1, columns)]
    meet(peers)

    shards = (proj_ref, out_ref)
    depth = proj_ref.shape[0]
    width = proj_ref.shape[1]
    out_depth, out_width = out_ref.shape

    def place(which, block_row, block_col, part=None):
        tall = depth if which == 0 else out_depth
        first = 0 if part is None else part * (tall // 2)
        size = tall if part is None else tall // 2
        if which == 0:
            return all_proj.at[
                pl.ds(pl.multiple_of(block_row * depth + first, 16), size),
                pl.ds(pl.multiple_of(block_col * width, width), width),
            ]
        return all_out.at[
            pl.ds(pl.multiple_of(block_row * out_depth + first, 16), size),
            pl.ds(pl.multiple_of(block_col * out_width, 128), out_width),
        ]

    pending = []

    def go(copy):
        copy.start()
        pending.append(copy)
        return copy

    part_copies = []
    for s in range(1, columns):
        target = lax.rem(col + s, columns)
        part_copies.append(
            go(
                remote(
                    maps_ref.at[target],
                    parts.at[s - 1],
                    part_send.at[s - 1],
                    part_recv.at[s - 1],
                    at_col(target),
                )
            )
        )
    line = {}

    def start_line(which):
        for s in range(1, rows):
            line[which, s] = go(
                remote(
                    shards[which],
                    place(which, row, col),
                    line_send.at[which, s - 1],
                    line_recv.at[which, s - 1],
                    at_row(lax.rem(row + s, rows)),
                )
            )

    start_line(0)
    own = []
    for which in range(2):
        own.append(
            pltpu.make_async_copy(shards[which], place(which, row, col), own_sem.at[which])
        )
        own[-1].start()

    if square:
        across = lax.rem(chip, 2)
        upward = chip // 2
        chip_x = upward * 2 + 1 - across
        chip_y = (1 - upward) * 2 + across
        chip_d = (1 - upward) * 2 + 1 - across
        senders = [chip_x, chip_y]
        targets = [chip_x, chip_y]
    else:
        targets = [lax.rem(chip + t, chips) for t in range(1, chips)]
        senders = [lax.rem(chip + chips - t, chips) for t in range(1, chips)]

    plane = {}
    pair = {}

    def to_pair(which, s, slot, source, target):
        pair[which, s, slot] = go(
            remote(
                source,
                target,
                pair_send.at[which, s, slot],
                pair_recv.at[which, s, slot],
                at_col(sibling),
            )
        )

    def spread(which, s):
        block_row = lax.rem(row + rows - s, rows)
        if s > 0:
            line[which, s].wait_recv()
            source = place(which, block_row, col)
        else:
            source = shards[which]
        for t, target in enumerate(targets):
            plane[which, s, t] = go(
                remote(
                    source,
                    place(which, block_row, col),
                    plane_send.at[which, s, t],
                    plane_recv.at[which, s, t],
                    at_col(target * 2 + core),
                )
            )
        to_pair(which, s, 0, source, place(which, block_row, col))

    def relay(which, s):
        block_row = lax.rem(row + rows - s, rows)
        for t, sender in enumerate(senders):
            plane[which, s, t].wait_recv()
            if square:
                onward = place(which, block_row, sender * 2 + core, t)
                plane[which, s, 2 + t] = go(
                    remote(
                        onward,
                        onward,
                        plane_send.at[which, s, 2 + t],
                        plane_recv.at[which, s, 2 + t],
                        at_col(targets[1 - t] * 2 + core),
                    )
                )
            here = place(which, block_row, sender * 2 + core)
            to_pair(which, s, 1 + t, here, here)

    def corner(which, s):
        if not square:
            return
        block_row = lax.rem(row + rows - s, rows)
        for t in range(2):
            plane[which, s, 2 + t].wait_recv()
        here = place(which, block_row, chip_d * 2 + core)
        to_pair(which, s, 3, here, here)

    steps = [(0, 0), (1, 0)]
    steps += [(which, s) for which in range(2) for s in range(1, rows)]
    for i, step in enumerate(steps):
        spread(*step)
        if i == 2:
            total = maps_ref[col].astype(jnp.float32)
            for s in range(1, columns):
                part_copies[s - 1].wait_recv()
                total = total + parts[s - 1].astype(jnp.float32)
            chunk[...] = total.astype(jnp.bfloat16)
            map_copies = []
            for s in range(1, columns):
                map_copies.append(
                    go(
                        remote(
                            chunk,
                            all_maps.at[col],
                            map_send.at[s - 1],
                            map_recv.at[s - 1],
                            at_col(lax.rem(col + s, columns)),
                        )
                    )
                )
            mine = pltpu.make_async_copy(chunk, all_maps.at[col], own_sem.at[2])
            mine.start()
        if i == 1:
            start_line(1)
        if i >= 1:
            relay(*steps[i - 1])
        if i >= 2:
            corner(*steps[i - 2])
    relay(*steps[-1])
    corner(*steps[-2])
    corner(*steps[-1])
    for key in pair:
        pair[key].wait_recv()
    for copy in map_copies:
        copy.wait_recv()
    for copy in own:
        copy.wait()
    mine.wait()
    for copy in pending:
        copy.wait_send()


def gather_weights(projection_weight, output_weight, maps):
    rows = lax.axis_size("row")
    columns = lax.axis_size("col")
    dma = pltpu.SemaphoreType.DMA
    slots = 4 if columns == 8 else columns // 2
    anywhere = pl.BlockSpec(memory_space=pl.ANY)
    return pl.pallas_call(
        functools.partial(gather_kernel, rows, columns),
        out_shape=(
            jax.ShapeDtypeStruct(
                (projection_weight.shape[0] * rows, projection_weight.shape[1] * columns),
                jnp.bfloat16,
            ),
            jax.ShapeDtypeStruct(
                (output_weight.shape[0] * rows, output_weight.shape[1] * columns), jnp.bfloat16
            ),
            jax.ShapeDtypeStruct(maps.shape, jnp.bfloat16),
        ),
        in_specs=[anywhere, anywhere, pl.BlockSpec(memory_space=pltpu.VMEM)],
        out_specs=(anywhere, anywhere, anywhere),
        scratch_shapes=[
            pltpu.VMEM((columns - 1,) + maps.shape[1:], jnp.bfloat16),
            pltpu.VMEM(maps.shape[1:], jnp.bfloat16),
            dma((3,)),
            dma((2, rows - 1)),
            dma((2, rows - 1)),
            dma((2, rows, slots)),
            dma((2, rows, slots)),
            dma((2, rows, slots)),
            dma((2, rows, slots)),
            dma((columns - 1,)),
            dma((columns - 1,)),
            dma((columns - 1,)),
            dma((columns - 1,)),
        ],
        compiler_params=pltpu.CompilerParams(
            collective_id=0, has_side_effects=True, vmem_limit_bytes=16 * 1024 * 1024
        ),
        name="gather_weights",
    )(projection_weight, output_weight, maps)


def share_kernel(columns, exchange, block_ref, all_ref, own_sem, send_sem, recv_sem):
    row = lax.axis_index("row")
    col = lax.axis_index("col")
    others = [lax.rem(col + s, columns) for s in range(1, columns)]
    meet([{"row": row, "col": other} for other in others])
    copies = []
    for s, other in enumerate(others):
        copies.append(
            remote(
                block_ref.at[other] if exchange else block_ref,
                all_ref.at[col],
                send_sem.at[s],
                recv_sem.at[s],
                {"row": row, "col": other},
            )
        )
        copies[-1].start()
    mine = pltpu.make_async_copy(
        block_ref.at[col] if exchange else block_ref, all_ref.at[col], own_sem
    )
    mine.start()
    mine.wait()
    for copy in copies:
        copy.wait()


def share(block, exchange, identity):
    columns = lax.axis_size("col")
    dma = pltpu.SemaphoreType.DMA
    shape = block.shape if exchange else (columns,) + block.shape
    return pl.pallas_call(
        functools.partial(share_kernel, columns, exchange),
        out_shape=jax.ShapeDtypeStruct(shape, block.dtype),
        in_specs=[pl.BlockSpec(memory_space=pl.ANY)],
        out_specs=pl.BlockSpec(memory_space=pl.ANY),
        scratch_shapes=[dma, dma((columns - 1,)), dma((columns - 1,))],
        compiler_params=pltpu.CompilerParams(
            collective_id=identity, has_side_effects=True, vmem_limit_bytes=16 * 1024 * 1024
        ),
        name="exchange" if exchange else "share",
    )(block)


def experts_kernel(
    columns,
    sending_ref,
    gate_ref,
    up_ref,
    down_ref,
    all_ref,
    gate,
    up,
    down,
    arrived,
    answer,
    load_sem,
    own_sem,
    send_sem,
    recv_sem,
    back_send,
    back_recv,
):
    row = lax.axis_index("row")
    col = lax.axis_index("col")
    chips = columns // 2
    core = lax.rem(col, 2)
    chip = col // 2
    meet([{"row": row, "col": lax.rem(col + s, columns)} for s in range(1, columns)])
    loads = [
        pltpu.make_async_copy(gate_ref, gate, load_sem.at[0]),
        pltpu.make_async_copy(up_ref, up, load_sem.at[1]),
        pltpu.make_async_copy(down_ref, down, load_sem.at[2]),
    ]
    for load in loads:
        load.start()
    if chips == 4:
        across = lax.rem(chip, 2)
        upward = chip // 2
        targets = [
            chip,
            upward * 2 + 1 - across,
            (1 - upward) * 2 + across,
            (1 - upward) * 2 + 1 - across,
        ]
        sources = targets
    else:
        targets = [lax.rem(chip + t, chips) for t in range(chips)]
        sources = [lax.rem(chip + chips - t, chips) for t in range(chips)]
    rows = sending_ref.shape[1]
    cap = rows // gate_ref.shape[0]

    def outward(g, other):
        target = targets[g] * 2 + other
        return remote(
            sending_ref.at[target],
            arrived.at[2 * g + core],
            send_sem.at[2 * g + other],
            recv_sem.at[2 * g + core],
            {"row": row, "col": target},
        )

    def inward(g, other):
        return remote(
            sending_ref.at[col],
            arrived.at[2 * g + other],
            send_sem.at[2 * g + other],
            recv_sem.at[2 * g + other],
            {"row": row, "col": targets[g] * 2 + other},
        )

    def back(g, other):
        return remote(
            answer.at[2 * g + other],
            all_ref.at[col],
            back_send.at[2 * g + other],
            back_recv.at[2 * g + core],
            {"row": row, "col": sources[g] * 2 + other},
        )

    def back_in(g, other):
        return remote(
            answer.at[2 * g + other],
            all_ref.at[targets[g] * 2 + other],
            back_send.at[2 * g + other],
            back_recv.at[2 * g + other],
            {"row": row, "col": targets[g] * 2 + other},
        )

    def members(g):
        return [1 - core] if g == 0 else [0, 1]

    def work(g):
        held = jnp.concatenate([arrived[2 * g], arrived[2 * g + 1]], axis=0)
        spot = lax.broadcasted_iota(jnp.int32, (2 * rows, 1), 0)
        spot = jnp.where(spot >= rows, spot - rows, spot)
        total = None
        for j in range(gate.shape[0]):
            gate_vals = jnp.dot(held, gate[j], preferred_element_type=jnp.float32)
            up_vals = jnp.dot(held, up[j], preferred_element_type=jnp.float32)
            mine = (spot >= j * cap) & (spot < (j + 1) * cap)
            hidden = jnp.where(mine, jnp.maximum(gate_vals, 0.0) * up_vals, 0.0)
            part = jnp.dot(
                hidden.astype(jnp.bfloat16), down[j], preferred_element_type=jnp.float32
            )
            total = part if total is None else total + part
        total = total.astype(jnp.bfloat16)
        answer[2 * g] = total[:rows]
        answer[2 * g + 1] = total[rows:]

    first = min(chips, 3)
    sent = []
    for g in list(range(1, first)) + [0]:
        for other in members(g):
            sent.append(outward(g, other))
            sent[-1].start()
    mine = pltpu.make_async_copy(sending_ref.at[col], arrived.at[core], own_sem.at[0])
    mine.start()
    for load in loads:
        load.wait()
    mine.wait()
    for g in range(chips):
        for other in members(g):
            inward(g, other).wait_recv()
        work(g)
        if g == 0:
            for late in range(first, chips):
                for other in members(late):
                    sent.append(outward(late, other))
                    sent[-1].start()
            kept = pltpu.make_async_copy(answer.at[core], all_ref.at[col], own_sem.at[1])
            kept.start()
        for other in members(g):
            sent.append(back(g, other))
            sent[-1].start()
    for g in range(chips):
        for other in members(g):
            back_in(g, other).wait_recv()
    kept.wait()
    for copy in sent:
        copy.wait_send()


def run_experts(sending, gate, up, down):
    columns = lax.axis_size("col")
    dma = pltpu.SemaphoreType.DMA
    anywhere = pl.BlockSpec(memory_space=pl.ANY)
    return pl.pallas_call(
        functools.partial(experts_kernel, columns),
        out_shape=jax.ShapeDtypeStruct(sending.shape, jnp.bfloat16),
        in_specs=[pl.BlockSpec(memory_space=pltpu.VMEM), anywhere, anywhere, anywhere],
        out_specs=anywhere,
        scratch_shapes=[
            pltpu.VMEM(gate.shape, jnp.bfloat16),
            pltpu.VMEM(up.shape, jnp.bfloat16),
            pltpu.VMEM(down.shape, jnp.bfloat16),
            pltpu.VMEM(sending.shape, jnp.bfloat16),
            pltpu.VMEM(sending.shape, jnp.bfloat16),
            dma((3,)),
            dma((2,)),
            dma((columns,)),
            dma((columns,)),
            dma((columns,)),
            dma((columns,)),
        ],
        compiler_params=pltpu.CompilerParams(
            collective_id=2, has_side_effects=True, vmem_limit_bytes=58 * 1024 * 1024
        ),
        name="run_experts",
    )(sending, gate, up, down)


def project_kernel(rows, attended_ref, packed_ref, parts_ref):
    depth = attended_ref.shape[1] // rows
    tall = packed_ref.shape[0] // rows
    half = depth // 2
    attended = attended_ref[...]
    sums = [None, None, None]
    for r in range(rows):
        mine = attended[:, r * depth : (r + 1) * depth]
        front = packed_ref[r * tall : r * tall + depth, :]
        side = packed_ref[r * tall + depth : (r + 1) * tall, :]
        pairs = ((mine, front), (mine[:, :half], side), (mine[:, half:], side))
        for i, (left, right) in enumerate(pairs):
            term = jnp.dot(left, right, preferred_element_type=jnp.float32)
            sums[i] = term if sums[i] is None else sums[i] + term
    for i in range(3):
        parts_ref[i] = sums[i]


def project_out(attended, packed, rows):
    vmem = pl.BlockSpec(memory_space=pltpu.VMEM)
    return pl.pallas_call(
        functools.partial(project_kernel, rows),
        out_shape=jax.ShapeDtypeStruct((3, attended.shape[0], packed.shape[1]), jnp.float32),
        in_specs=[vmem, vmem],
        out_specs=vmem,
        compiler_params=pltpu.CompilerParams(vmem_limit_bytes=24 * 1024 * 1024),
        name="project_out",
    )(attended, packed)


def local(
    hidden_input,
    lengths,
    prompt_adapter,
    routes,
    attention_norm_gain,
    expert_norm_gain,
    projection_weight,
    output_weight,
    router,
    adapter_projection_down,
    adapter_projection_up,
    adapter_output_down,
    adapter_output_up,
    expert_gate_weight,
    expert_up_weight,
    expert_down_weight,
):
    token_rows = hidden_input.shape[0]
    model_width = hidden_input.shape[1]
    columns = lax.axis_size("col")
    row_index = lax.axis_index("row")
    col_index = lax.axis_index("col")
    lengths_row = lax.dynamic_index_in_dim(lengths, row_index, 0, keepdims=False)
    adapter_row = lax.dynamic_index_in_dim(prompt_adapter, row_index, 0, keepdims=False)
    tok_index = col_index * token_rows + jnp.arange(token_rows, dtype=jnp.int32)
    prompt_of, within_prompt, token_positions = prompt_layout(lengths_row, tok_index)
    adapter_count = adapter_projection_down.shape[0]

    def choose_experts(table):
        return sum(
            jnp.where(
                (adapter_row == col_index * adapter_count + a)[:, None, None],
                table[a][None].astype(jnp.float32),
                0.0,
            )
            for a in range(adapter_count)
        )

    tables = (
        adapter_projection_down,
        adapter_projection_up,
        adapter_output_down,
        adapter_output_up,
    )
    chosen = jnp.concatenate(
        [choose_experts(table).astype(jnp.bfloat16) for table in tables], axis=2
    )
    prompts, rank, map_width = chosen.shape
    splits = columns // prompts
    chosen = (
        chosen.reshape(prompts, rank, splits, map_width // splits)
        .transpose(0, 2, 1, 3)
        .reshape(columns, rank, map_width // splits)
    )
    out_depth, out_width = output_weight.shape
    paired = out_width == 192
    if paired:
        side = output_weight[:, 128:]
        packed = jnp.concatenate(
            [
                output_weight[:, :128],
                jnp.concatenate([side[: out_depth // 2], side[out_depth // 2 :]], axis=1),
            ],
            axis=0,
        )
    else:
        packed = jnp.pad(output_weight, ((0, 0), (0, -out_width % 128)))
    qkv_full, out_packed, all_maps = gather_weights(projection_weight, packed, chosen)
    all_maps = (
        all_maps.reshape(prompts, splits, rank, map_width // splits)
        .transpose(0, 2, 1, 3)
        .reshape(prompts, rank, map_width)
    )
    cuts = []
    for table in tables:
        cuts.append((cuts[-1] if cuts else 0) + table.shape[2])
    projection_down_map, projection_up_map, output_down_map, output_up_map = jnp.split(
        all_maps, cuts[:-1], axis=2
    )
    normalized = rms_scaled(hidden_input, attention_norm_gain)
    projection_all = jnp.dot(normalized, qkv_full, preferred_element_type=jnp.float32)
    projection_all = projection_all + adapter_scale * adapter_change(
        normalized, within_prompt, projection_down_map, projection_up_map
    )
    query_slice = apply_rotary(
        projection_all[:, : QUERY_HEADS * HEAD_SIZE].reshape(token_rows, QUERY_HEADS, HEAD_SIZE),
        token_positions,
    ).astype(jnp.bfloat16)
    key_slice = apply_rotary(
        projection_all[:, QUERY_HEADS * HEAD_SIZE : (QUERY_HEADS + KEY_HEADS) * HEAD_SIZE].reshape(
            token_rows, KEY_HEADS, HEAD_SIZE
        ),
        token_positions,
    ).astype(jnp.bfloat16)
    value_slice = projection_all[:, (QUERY_HEADS + KEY_HEADS) * HEAD_SIZE :].astype(jnp.bfloat16)
    flattened_keys = key_slice.reshape(token_rows, KEY_HEADS * HEAD_SIZE)
    grouped = (
        query_slice.reshape(token_rows, KEY_HEADS, QUERY_PER_KEY, HEAD_SIZE)
        .transpose(1, 2, 0, 3)
        .reshape(KEY_HEADS, QUERY_PER_KEY * token_rows, HEAD_SIZE)
    )
    query_index = jnp.tile(tok_index, QUERY_PER_KEY)
    query_prompt = jnp.tile(prompt_of, QUERY_PER_KEY)
    shared = share(jnp.concatenate([flattened_keys, value_slice], axis=1), False, 1)
    shared = shared.reshape(columns * token_rows, 2 * KEY_HEADS * HEAD_SIZE)
    segments = (shared[:, : KEY_HEADS * HEAD_SIZE], shared[:, KEY_HEADS * HEAD_SIZE :])
    best_experts = jnp.full((KEY_HEADS, QUERY_PER_KEY * token_rows), -1e30, jnp.float32)
    segment_length = segments[0].shape[0]
    key_lines = segments[0].reshape(segment_length, KEY_HEADS, HEAD_SIZE).transpose(1, 0, 2)
    value_lines = segments[1].reshape(segment_length, KEY_HEADS, HEAD_SIZE).transpose(1, 0, 2)
    key_index = jnp.arange(segment_length, dtype=jnp.int32)
    key_prompt = prompt_layout(lengths_row, key_index)[0]
    allowed = (key_prompt[None, :] == query_prompt[:, None]) & (
        key_index[None, :] <= query_index[:, None]
    )
    scores = jnp.einsum(
        "hqd,hkd->hqk", grouped, key_lines, preferred_element_type=jnp.float32
    ) * HEAD_SIZE ** (-0.5)
    masked = jnp.where(allowed[None], scores, -1e30)
    fresh = jnp.maximum(best_experts, jnp.max(masked, axis=-1))
    weights = jnp.where(allowed[None], jnp.exp(scores - fresh[..., None]), 0.0)
    running_new = jnp.sum(weights, axis=-1)
    accum_new = jnp.einsum(
        "hqk,hkd->hqd",
        weights.astype(jnp.bfloat16),
        value_lines,
        preferred_element_type=jnp.float32,
    )
    mixed_output = accum_new / running_new[..., None]
    attention_result = (
        mixed_output.reshape(KEY_HEADS, QUERY_PER_KEY, token_rows, HEAD_SIZE)
        .transpose(2, 0, 1, 3)
        .reshape(token_rows, QUERY_HEADS * HEAD_SIZE)
        .astype(jnp.bfloat16)
    )
    row_count = lax.axis_size("row")
    if paired:
        parts = project_out(attention_result, out_packed, row_count).reshape(
            3, token_rows, columns, 128
        )
        front = parts[0]
        halves = [parts[1][:, :, :64], parts[2][:, :, 64:]]
        projected_rows = jnp.concatenate([front, halves[0] + halves[1]], axis=2)
    else:
        projected_rows = jnp.dot(
            attention_result, out_packed, preferred_element_type=jnp.float32
        ).reshape(token_rows, columns, packed.shape[1])[:, :, :out_width]
    projected_rows = projected_rows.reshape(token_rows, model_width)
    projected_rows = projected_rows + adapter_scale * adapter_change(
        attention_result, within_prompt, output_down_map, output_up_map
    )
    residual = (hidden_input.astype(jnp.float32) + projected_rows).astype(jnp.bfloat16)
    normed_two = rms_scaled(residual, expert_norm_gain)
    logits = jnp.dot(normed_two, router, preferred_element_type=jnp.float32)
    squashed = jax.nn.sigmoid(
        jnp.sum(
            jnp.where(
                routes[:, :, None] == jnp.arange(router.shape[1], dtype=jnp.int32)[None, None, :],
                logits[:, None, :],
                0.0,
            ),
            axis=2,
        )
    )
    mixing = squashed / jnp.sum(squashed, axis=1, keepdims=True)
    expert_total = router.shape[1]
    local_experts = expert_gate_weight.shape[0]
    flat_routes = routes.reshape(-1)
    slots = route_slots(flat_routes, expert_total)
    spots = (flat_routes * CAP + slots).reshape(routes.shape)
    spot_index = jnp.arange(expert_total * CAP, dtype=jnp.int32)
    marked = spots[:, :, None] == spot_index[None, None, :]
    dispatch = jnp.any(marked, axis=1).astype(jnp.bfloat16)
    sending = jnp.einsum(
        "tj,td->jd", dispatch, normed_two, preferred_element_type=jnp.float32
    ).astype(jnp.bfloat16)
    sending = sending.reshape(columns, local_experts * CAP, model_width)
    returned = run_experts(
        sending, expert_gate_weight, expert_up_weight, expert_down_weight
    ).reshape(expert_total * CAP, model_width)
    mix = jnp.sum(jnp.where(marked, mixing[:, :, None], 0.0), axis=1)
    mix_high = mix.astype(jnp.bfloat16)
    mix_low = (mix - mix_high.astype(jnp.float32)).astype(jnp.bfloat16)
    combined = jnp.dot(mix_high, returned, preferred_element_type=jnp.float32) + jnp.dot(
        mix_low, returned, preferred_element_type=jnp.float32
    )
    return (residual.astype(jnp.float32) + combined).astype(jnp.bfloat16)


def solution(mesh):
    placed = (
        P(("row", "col"), None),
        P(),
        P(),
        P(("row", "col"), None),
        P(),
        P(),
        P("row", "col"),
        P("row", "col"),
        P(),
        P("col", None, None),
        P("col", None, None),
        P("col", None, None),
        P("col", None, None),
        P("col", None, None),
        P("col", None, None),
        P("col", None, None),
    )
    return jax.shard_map(
        local, mesh=mesh, in_specs=placed, out_specs=P(("row", "col"), None), check_vma=False
    )
```
